256 devices in a mesh: section: 2 (over x_hi), dp: 32 (over z, x_lo, core), tensor: 4 (over y).
Axes of the slice: x: 4 (x_hi: 2, x_lo: 2; x = x_hi * 2 + x_lo), y: 4, z: 8, core: 2. Of those that a mesh axis runs over, the one named last changes fastest.
Arguments:
- left: bfloat16 [2, 16384, 8192], P('section', 'dp', 'tensor'), may hold values from -6 to 6
- weight: bfloat16 [2, 8192, 5120], P('section', ('tensor', 'dp')), may hold values from -0.0625 to 0.0625
- base: bfloat16 [2, 16384, 5120], P('section', 'dp', 'tensor'), may hold values from -6 to 6
- expo: int32 [2, 128, 40], P('section', 'dp', 'tensor'), may hold values from -7 to 2
- perm: int32 [2, 32, 4], P('section', 'dp'), may hold values from 0 to 3, each once within a row
Outputs:
- received: float32 [2, 16384, 5120], P('section', ('dp', 'tensor'))
The draws below stay inside these ranges and needn't reach their ends.
Inputs may be any that keep to these rules, and one draw needn't show every extreme that they name: Each row of perm holds every number from 0 to 3 once.
All inputs are finite; a program needn't handle non-finite values.
Results may differ from the reference program's by a relative error of at most 0.01.
Values may be sent and summed in bfloat16 or wider, within the bound.
No kernel may reach another device: no remote copies, remote signals or barrier semaphores. Data moves between devices by JAX's collectives and lax.ppermute only.
A program may use at most 128 MiB of HBM per device.

```python
import math
import jax
import jax.numpy as jnp
from jax import lax

D = 5120
C_ALL = 8192
TILE = 128
TOKENS = 16384
BLK = 4
N_SECTION = 2
N_DP = 32
N_TENSOR = 4


def with_ends(entries, own_key, low, top_value):
    place = [jax.random.randint(jax.random.fold_in(own_key, axis), (), 0, length) for axis, length in enumerate(entries.shape)]
    widest = entries.shape.index(max(entries.shape))
    neighbour = place[:widest] + [(place[widest] + 1) % entries.shape[widest]] + place[widest + 1:]
    return entries.at[tuple(place)].set(low).at[tuple(neighbour)].set(top_value)


def level_of(stream_key, extent, pieces, low, high):
    loudness = 1.0
    for dim, blocks in pieces:
        steps = jax.random.uniform(jax.random.fold_in(jax.random.fold_in(stream_key, 6), dim), (blocks,), jnp.float32, low / len(pieces), high / len(pieces))
        loudness = loudness * jnp.repeat(jnp.exp(steps), extent[dim] // blocks).reshape((-1,) + (1,) * (len(extent) - 1 - dim))
    return loudness


def gaussian(stream_key, extent, deviation, limit, pieces=(), kind=jnp.bfloat16):
    factor_of = level_of(stream_key, extent, pieces, -0.22, 0.18) if pieces else 1.0
    drawn = jax.random.normal(stream_key, extent, jnp.float32) * deviation * factor_of
    return jnp.minimum(jnp.maximum(drawn, -limit), limit).astype(kind)


def setup_inputs(seed: int = 0) -> dict:
    seeds = jax.random.split(jax.random.key(seed), 6)
    return {
        "left": gaussian(seeds[0], (N_SECTION, TOKENS, C_ALL), 1.0, 6.0, ((0, 2), (1, 32), (2, 4))),
        "weight": gaussian(seeds[1], (N_SECTION, C_ALL, D), C_ALL ** -0.5, 0.0625, ((0, 2), (1, 128))),
        "base": gaussian(seeds[2], (N_SECTION, TOKENS, D), 1.0, 6.0, ((0, 2), (1, 32), (2, 4))),
        "expo": with_ends(jax.random.randint(seeds[3], (N_SECTION, TOKENS // TILE, D // TILE), -7, 3), jax.random.fold_in(seeds[3], 1), -7, 2).astype(jnp.int32),
        "perm": jax.vmap(lambda own: jax.random.permutation(own, BLK))(jax.random.split(seeds[4], N_SECTION * N_DP)).reshape((N_SECTION, N_DP, BLK)).astype(jnp.int32),
    }


def hadamard(size):
    index = jnp.arange(size, dtype=jnp.int32)
    common = jnp.bitwise_and(index[:, None], index[None, :])
    parity = jnp.zeros((size, size), jnp.int32)
    for shift_bit in range(size.bit_length() - 1):
        parity = parity + jnp.bitwise_and(jnp.right_shift(common, shift_bit), 1)
    signs = 1 - 2 * jnp.bitwise_and(parity, 1)
    return signs.astype(jnp.float32) / math.sqrt(size)

def rotate(values, table):
    size = table.shape[0]
    rows, cols = values.shape
    tiles = values.reshape(rows // size, size, cols // size, size)
    turned = jnp.einsum('aibj,jk->aibk', tiles, table, precision=lax.Precision.HIGHEST)
    return turned.reshape(rows, cols)

def quantize(values, exponent, table):
    size = table.shape[0]
    rows, cols = values.shape
    turned = rotate(values, table).reshape(rows // size, size, cols // size, size)
    scaled = turned * jnp.exp2(-exponent.astype(jnp.float32))[:, None, :, None]
    return jnp.clip(scaled.astype(jnp.bfloat16), -448.0, 448.0).reshape(rows, cols)

def restore(quant, exponent, table):
    size = table.shape[0]
    rows, cols = quant.shape
    values = quant.astype(jnp.float32).reshape(rows // size, size, cols // size, size)
    values = values * jnp.exp2(exponent.astype(jnp.float32))[:, None, :, None]
    return rotate(values.reshape(rows, cols), table)

def reference(left, weight, base, expo, perm):
    table = hadamard(TILE)
    width = C_ALL // N_TENSOR
    feat = D // N_TENSOR
    results = []
    for section_index in range(N_SECTION):
        total = jnp.zeros((TOKENS, D), jnp.float32)
        for group in range(N_TENSOR):
            piece = jnp.dot(left[section_index][:, group * width:(group + 1) * width], weight[section_index][group * width:(group + 1) * width, :], preferred_element_type=jnp.float32)
            piece = piece.at[:, group * feat:(group + 1) * feat].add(base[section_index][:, group * feat:(group + 1) * feat].astype(jnp.float32))
            total = total + piece.astype(jnp.bfloat16).astype(jnp.float32)
        quant = quantize(total, expo[section_index], table)
        restored = restore(quant, expo[section_index], table)
        blocks = restored.reshape(N_DP, BLK, TILE, D)
        groups = jnp.arange(N_DP, dtype=jnp.int32)[:, None]
        placed = jnp.zeros_like(blocks).at[groups, perm[section_index]].set(blocks)
        results.append(placed.reshape(TOKENS, D))
    return jnp.stack([results[1], results[0]])
```

```python
import functools
import math

import jax
import jax.numpy as jnp
import numpy as np
from jax import lax
from jax.experimental import pallas as pl
from jax.experimental.pallas import tpu as pltpu
from jax.sharding import PartitionSpec as P

TILE = 128
N_T = 4
N_Z = 8
GROUP = 4
DP = N_Z * GROUP
WIDE = 640
DEPTH = 2048
FULL = 5120
ROOT = 1.0 / math.sqrt(TILE)
VMEM_LIMIT = 48 * 1024 * 1024
MIB = 1024 * 1024


def signs():
    index = np.arange(TILE)
    common = index[:, None] & index[None, :]
    parity = np.zeros((TILE, TILE), np.int64)
    for shift in range(7):
        parity += (common >> shift) & 1
    return jnp.asarray(1 - 2 * (parity & 1), jnp.bfloat16)


def call(body, out_shape, n_scalar, in_specs, out_specs, grid=(1,), scratch=(), cost=None):
    return pl.pallas_call(
        body,
        out_shape=out_shape,
        grid_spec=pltpu.PrefetchScalarGridSpec(
            num_scalar_prefetch=n_scalar,
            grid=grid,
            in_specs=in_specs,
            out_specs=out_specs,
            scratch_shapes=scratch,
        ),
        compiler_params=pltpu.CompilerParams(vmem_limit_bytes=VMEM_LIMIT),
        cost_estimate=cost,
    )


def whole(shape):
    return pl.BlockSpec(shape, lambda *_: (0,) * len(shape))


def bf16(*shape):
    return jax.ShapeDtypeStruct(shape, jnp.bfloat16)


def split_weight_body(sc, w_ref, *outs):
    x, c = sc[1], sc[2]
    for p, out in enumerate(outs):
        px, pc = x ^ (p >> 1), c ^ (p & 1)
        for u in range(2):
            start = pl.multiple_of((2 * pc + u) * 2 * WIDE + px * WIDE, 128)
            out[:, u * WIDE : (u + 1) * WIDE] = w_ref[:, pl.ds(start, WIDE)]


def split_weight(sc, weight):
    rows = weight.shape[0]
    return call(
        split_weight_body,
        [bf16(rows, 2 * WIDE)] * GROUP,
        1,
        [whole((rows, FULL))],
        [whole((rows, 2 * WIDE))] * GROUP,
        cost=pl.CostEstimate(flops=0, bytes_accessed=4 * rows * FULL, transcendentals=0),
    )(sc, weight)


def join_weight_body(sc, *refs):
    pieces, outs = refs[:GROUP], refs[GROUP:]
    own = sc[1] * 2 + sc[2]
    rows = pieces[0].shape[0]
    for p, piece in enumerate(pieces):
        start = pl.multiple_of((own ^ p) * rows, rows)
        for u, out in enumerate(outs):
            out[pl.ds(start, rows), :] = piece[:, u * WIDE : (u + 1) * WIDE]


def join_weight(sc, pieces):
    rows = pieces[0].shape[0]
    return call(
        join_weight_body,
        [bf16(GROUP * rows, WIDE)] * 2,
        1,
        [whole((rows, 2 * WIDE))] * GROUP,
        [whole((GROUP * rows, WIDE))] * 2,
        cost=pl.CostEstimate(flops=0, bytes_accessed=16 * rows * WIDE * 2, transcendentals=0),
    )(sc, *pieces)


def order_left_body(sc, left_ref, near_ref, far_ref, near_out, far_out):
    near_out[0, :, :DEPTH] = left_ref[...]
    far_out[0, :, :DEPTH] = left_ref[...]
    near_out[0, :, DEPTH:] = near_ref[...]
    far_out[0, :, DEPTH:] = far_ref[...]


def order_left(sc, left, base):
    def block(k, sc):
        want = (sc[0] + k) % N_T
        return sum(jnp.where(sc[4 + j] == want, j, 0) for j in range(N_T))

    return call(
        order_left_body,
        [bf16(N_T, TILE, DEPTH + WIDE)] * 2,
        1,
        [
            pl.BlockSpec((TILE, DEPTH), lambda k, sc: (block(k, sc), 0)),
            pl.BlockSpec((TILE, WIDE), lambda k, sc: (block(k, sc), sc[1])),
            pl.BlockSpec((TILE, WIDE), lambda k, sc: (block(k, sc), 1 - sc[1])),
        ],
        [pl.BlockSpec((1, TILE, DEPTH + WIDE), lambda k, sc: (k, 0, 0))] * 2,
        grid=(N_T,),
        cost=pl.CostEstimate(flops=0, bytes_accessed=10 * MIB, transcendentals=0),
    )(sc, left, base, base)


def product_body(chunk, n, sc, *refs):
    lefts, w_ref, outs = refs[:n], refs[n], refs[n + 1 :]
    k = pl.program_id(0)
    mine = jnp.where((sc[0] == 2 * sc[2] + chunk), 1.0, 0.0)
    for i in range(n):
        total = jnp.dot(lefts[i][0, :, :DEPTH], w_ref[...], preferred_element_type=jnp.float32)
        total = total + lefts[i][0, :, DEPTH:].astype(jnp.float32) * mine
        total = total.astype(jnp.bfloat16)
        for kk, out in enumerate(outs):

            @pl.when(k == kk)
            def _(out=out, i=i, total=total):
                out[i] = total


def product(sc, chunk, lefts, weight):
    n = len(lefts)
    return call(
        functools.partial(product_body, chunk, n),
        [bf16(n, TILE, WIDE)] * N_T,
        1,
        [pl.BlockSpec((1, TILE, DEPTH + WIDE), lambda k, sc: (k, 0, 0))] * n + [whole((DEPTH, WIDE))],
        [whole((n, TILE, WIDE))] * N_T,
        grid=(N_T,),
        cost=pl.CostEstimate(
            flops=2 * n * N_T * TILE * DEPTH * WIDE, bytes_accessed=(3 * n + 3) * MIB, transcendentals=0
        ),
    )(sc, *lefts, weight)


def turn_body(n, h_ref, *refs):
    parts, outs = refs[:N_T], refs[N_T:]
    for i, out in enumerate(outs):
        for j in range(WIDE // TILE):
            cols = slice(j * TILE, (j + 1) * TILE)
            total = jnp.dot(parts[0][i, :, cols], h_ref[...], preferred_element_type=jnp.float32)
            for part in parts[1:]:
                total += jnp.dot(part[i, :, cols], h_ref[...], preferred_element_type=jnp.float32)
            out[:, cols] = (total * ROOT).astype(jnp.bfloat16)


def turn(table, parts):
    n = parts[0].shape[0]
    return call(
        functools.partial(turn_body, n),
        [bf16(TILE, WIDE)] * n,
        0,
        [whole((TILE, TILE))] + [whole((n, TILE, WIDE))] * N_T,
        [whole((TILE, WIDE))] * n,
        cost=pl.CostEstimate(
            flops=8 * n * TILE * TILE * WIDE, bytes_accessed=n * MIB, transcendentals=0
        ),
    )(table, *parts)


def finish_body(sc, lim, h_ref, *refs):
    pieces, out = refs[:-1], refs[-1]
    x, c = sc[1], sc[2]
    for p in range(GROUP):
        for u in range(2):
            piece = pieces[2 * p + u]
            first = (2 * (c ^ (p & 1)) + u) * 10 + (x ^ (p >> 1)) * 5
            for j in range(WIDE // TILE):
                top = lim[first + j]
                value = piece[:, j * TILE : (j + 1) * TILE].astype(jnp.float32)
                value = jnp.clip(value, -top, top).astype(jnp.bfloat16)
                value = jnp.dot(value, h_ref[...], preferred_element_type=jnp.float32) * ROOT
                out[:, pl.ds(pl.multiple_of((first + j) * TILE, TILE), TILE)] = value


def finish(sc, lim, table, pieces):
    return call(
        finish_body,
        jax.ShapeDtypeStruct((TILE, FULL), jnp.float32),
        2,
        [whole((TILE, TILE))] + [whole((TILE, WIDE))] * len(pieces),
        whole((TILE, FULL)),
        cost=pl.CostEstimate(flops=2 * TILE * TILE * FULL, bytes_accessed=4 * MIB, transcendentals=0),
    )(sc, lim, table, *pieces)


def swap(value, offset):
    return lax.ppermute(value, "dp", [(i, i ^ offset) for i in range(DP)])


def cross(value, offset):
    pairs = [(s * DP + i, (1 - s) * DP + (i ^ offset)) for s in range(2) for i in range(DP)]
    return lax.ppermute(value, ("section", "dp"), pairs)


def along_y(value, steps):
    return lax.ppermute(value, "tensor", [(i, (i + steps) % N_T) for i in range(N_T)])


def gather_z(block):
    groups = [[z * GROUP + m for z in range(N_Z)] for m in range(GROUP)]
    return lax.all_gather(block, "dp", axis=0, tiled=True, axis_index_groups=groups)


def limits(expo, perm):
    here = lax.axis_index("tensor")
    other = 1 - lax.axis_index("section")
    top = 448.0 * jnp.exp2(expo.astype(jnp.float32))
    packed = jnp.concatenate([top, perm.astype(jnp.float32)[:, None]], axis=1)
    everyone = lax.all_gather(packed, ("section", "tensor"), axis=0).reshape(2, N_T, N_T, 11)
    theirs = lax.dynamic_index_in_dim(everyone, other, 0, keepdims=False)
    hit = theirs[:, :, 10] == here.astype(jnp.float32)
    return jnp.sum(jnp.where(hit[:, :, None], theirs[:, :, :10], 0.0), axis=1).reshape(-1)


def shards(left, weight, base, expo, perm):
    table = signs()
    dp = lax.axis_index("dp")
    sc = jnp.concatenate(
        [
            jnp.stack([lax.axis_index("tensor"), (dp // 2) % 2, dp % 2, dp // GROUP]).astype(jnp.int32),
            perm[0, 0],
        ]
    )
    pieces = split_weight(sc, weight[0])
    blocks = join_weight(sc, [pieces[0]] + [swap(pieces[p], p) for p in range(1, GROUP)])
    near, far = order_left(sc, left[0], base[0])
    far_x = swap(far, 2)
    near_c = swap(near, 1)
    far_xc = swap(far_x, 1)
    lim = limits(expo[0], perm[0, 0])
    arrived = {}
    for chunk in range(2):
        w = gather_z(blocks[chunk])
        for lefts, offsets in (((near, near_c), (0, 1)), ((far_x, far_xc), (2, 3))):
            parts = product(sc, chunk, lefts, w)
            parts = [parts[0]] + [along_y(parts[k], k) for k in range(1, N_T)]
            for offset, turned in zip(offsets, turn(table, parts)):
                arrived[offset, chunk] = cross(turned, offset)
    ordered = [arrived[p, u] for p in range(GROUP) for u in range(2)]
    return finish(sc, lim, table, ordered)[None]


def solution(mesh):
    in_specs = (
        P("section", "dp", "tensor"),
        P("section", ("tensor", "dp"), None),
        P("section", "dp", "tensor"),
        P("section", "dp", "tensor"),
        P("section", "dp", None),
    )
    out_specs = P("section", ("dp", "tensor"), None)
    return jax.shard_map(shards, mesh=mesh, in_specs=in_specs, out_specs=out_specs, check_vma=False)
```

```python
import functools
import math

import jax
import jax.numpy as jnp
import numpy as np
from jax import lax
from jax.experimental import pallas as pl
from jax.experimental.pallas import tpu as pltpu
from jax.sharding import PartitionSpec as P

TILE = 128
N_T = 4
N_Z = 8
GROUP = 4
DP = N_Z * GROUP
WIDE = 640
DEPTH = 2048
FULL = 5120
ROOT = 1.0 / math.sqrt(TILE)
MORE = 16
BOTH = 2 * WIDE
BIG = 60 * 1024 * 1024
VMEM_LIMIT = 20 * 1024 * 1024
MIB = 1024 * 1024


def signs():
    index = np.arange(TILE)
    common = index[:, None] & index[None, :]
    parity = np.zeros((TILE, TILE), np.int64)
    for shift in range(7):
        parity += (common >> shift) & 1
    return jnp.asarray(1 - 2 * (parity & 1), jnp.bfloat16)


def call(body, out_shape, n_scalar, in_specs, out_specs, grid=(1,), scratch=(), cost=None, vmem=VMEM_LIMIT):
    return pl.pallas_call(
        body,
        out_shape=out_shape,
        grid_spec=pltpu.PrefetchScalarGridSpec(
            num_scalar_prefetch=n_scalar,
            grid=grid,
            in_specs=in_specs,
            out_specs=out_specs,
            scratch_shapes=scratch,
        ),
        compiler_params=pltpu.CompilerParams(vmem_limit_bytes=vmem),
        cost_estimate=cost,
    )


def local(body, out_shape, n_in, smem=0, scratch=(), cost=None):
    vmem = pl.BlockSpec(memory_space=pltpu.VMEM)
    scalar = pl.BlockSpec(memory_space=pltpu.SMEM)
    return pl.pallas_call(
        body,
        out_shape=out_shape,
        in_specs=[scalar] * smem + [vmem] * n_in,
        out_specs=[vmem] * len(out_shape) if isinstance(out_shape, list) else vmem,
        scratch_shapes=scratch,
        compiler_params=pltpu.CompilerParams(vmem_limit_bytes=VMEM_LIMIT),
        cost_estimate=cost,
    )


def cost_of(flops, moved):
    return pl.CostEstimate(flops=flops // 64, bytes_accessed=moved // 64, transcendentals=0)


def bf16(*shape):
    return jax.ShapeDtypeStruct(shape, jnp.bfloat16)


def split_weight_body(sc, *refs):
    for w_ref, out in zip(refs[:GROUP], refs[GROUP:]):
        out[...] = w_ref[...]


def split_weight(sc, weight):
    rows = weight.shape[0]

    def spec(p):
        return pl.BlockSpec(
            (rows, WIDE), lambda u, sc: (0, (2 * (sc[2] ^ (p & 1)) + u) * 2 + (sc[1] ^ (p >> 1)))
        )

    return call(
        split_weight_body,
        [bf16(rows, 2 * WIDE)] * GROUP,
        1,
        [spec(p) for p in range(GROUP)],
        [pl.BlockSpec((rows, WIDE), lambda u, sc: (0, u))] * GROUP,
        grid=(2,),
        cost=cost_of(0, 4 * rows * FULL),
        vmem=BIG,
    )(sc, *[weight] * GROUP)


def join_weight_body(sc, own_ref, other_ref, out):
    rows = own_ref.shape[0]
    for p, piece in enumerate((own_ref, other_ref)):
        out[pl.ds(pl.multiple_of((sc[2] ^ p) * rows, rows), rows), :] = piece[...]


def join_weight(sc, pieces):
    rows = pieces[0].shape[0]
    return local(
        join_weight_body, bf16(2 * rows, BOTH), 2, smem=1, cost=cost_of(0, 8 * rows * BOTH)
    )(sc, *pieces)


def order_left_body(sc, left_ref, base_ref, *outs):
    rows = TILE // len(outs)
    for i, out in enumerate(outs):
        part = pl.ds(i * rows, rows)
        for j in range(N_Z):
            start = pl.multiple_of(((sc[3] + j) % N_Z) * (DEPTH // N_Z), DEPTH // N_Z)
            out[0, :, j * (DEPTH // N_Z) : (j + 1) * (DEPTH // N_Z)] = left_ref[part, pl.ds(start, DEPTH // N_Z)]
        out[0, :, DEPTH:] = base_ref[part, :]


def order_left(sc, left, base, other, halves):
    def block(k, sc):
        want = (sc[0] + k) % N_T
        return sum(jnp.where(sc[4 + j] == want, j, 0) for j in range(N_T))

    def half(sc):
        return 1 - sc[1] if other else sc[1]

    rows = TILE // halves
    return call(
        order_left_body,
        [bf16(N_T, rows, DEPTH + WIDE)] * halves,
        1,
        [
            pl.BlockSpec((TILE, DEPTH), lambda k, sc: (block(k, sc), 0)),
            pl.BlockSpec((TILE, WIDE), lambda k, sc: (block(k, sc), half(sc))),
        ],
        [pl.BlockSpec((1, rows, DEPTH + WIDE), lambda k, sc: (k, 0, 0))] * halves,
        grid=(N_T,),
        cost=cost_of(0, 6 * MIB),
        vmem=BIG,
    )(sc, left, base)


def product_body(first, sc, *refs):
    if first:
        top, left, blocks, w, outs = refs[0], refs[1], refs[2 : 2 + 2 * N_Z], refs[-1], refs[-1 - N_T : -1]
        rows = DEPTH // N_Z // 2
        for j in range(N_Z):
            for side in range(2):
                start = pl.multiple_of((2 * j + (sc[1] ^ side)) * rows, rows)
                w[pl.ds(start, rows), :] = blocks[2 * j + side][...]
        for k in range(N_T):
            outs[k][TILE:, :] = top[k]
    else:
        left, w, outs = refs[0], refs[1], refs[2:]
    for k in range(0, N_T, 2):
        a = left[k : k + 2, :, :DEPTH].reshape(2 * TILE, DEPTH)
        b = left[k : k + 2, :, DEPTH:].reshape(2 * TILE, WIDE).astype(jnp.float32)
        for u in range(2):
            cols = slice(u * WIDE, (u + 1) * WIDE)
            mine = jnp.where((sc[0] == 2 * sc[2] + u), 1.0, 0.0)
            total = jnp.dot(a, w[:, cols], preferred_element_type=jnp.float32)
            total = (total + b * mine).astype(jnp.bfloat16)
            outs[k][:TILE, cols] = total[:TILE]
            outs[k + 1][:TILE, cols] = total[TILE:]


PRODUCT_COST = cost_of(2 * N_T * TILE * DEPTH * BOTH, 8 * MIB)


def first_product(sc, top, left, blocks):
    outs = local(
        functools.partial(product_body, True),
        [bf16(TILE + MORE, BOTH)] * N_T + [bf16(DEPTH, BOTH)],
        2 + len(blocks),
        smem=1,
        cost=PRODUCT_COST,
    )(sc, top, left, *blocks)
    return outs[:N_T], outs[N_T]


def product(sc, left, weight):
    return local(
        functools.partial(product_body, False), [bf16(TILE, BOTH)] * N_T, 2, smem=1, cost=PRODUCT_COST
    )(sc, left, weight)


def add_body(a_ref, b_ref, out):
    out[...] = (a_ref[...].astype(jnp.float32) + b_ref[...].astype(jnp.float32)).astype(jnp.bfloat16)


def add(a, b):
    return local(add_body, bf16(*a.shape), 2, cost=cost_of(a.size, 6 * a.size))(a, b)


def turn_body(h_ref, *refs):
    parts, out = refs[:-1], refs[-1]
    for j in range(BOTH // TILE):
        cols = slice(j * TILE, (j + 1) * TILE)
        total = jnp.dot(parts[0][:TILE, cols], h_ref[...], preferred_element_type=jnp.float32)
        for part in parts[1:]:
            total += jnp.dot(part[:TILE, cols], h_ref[...], preferred_element_type=jnp.float32)
        out[:TILE, cols] = (total * ROOT).astype(jnp.bfloat16)
    if out.shape[0] > TILE:
        total = parts[0][TILE:, :].astype(jnp.float32)
        for part in parts[1:]:
            total += part[TILE:, :].astype(jnp.float32)
        out[TILE:, :] = total.astype(jnp.bfloat16)


def turn(table, parts):
    rows = parts[0].shape[0]
    return local(
        turn_body,
        bf16(rows, BOTH),
        1 + len(parts),
        cost=cost_of(8 * TILE * TILE * BOTH, MIB),
    )(table, *parts)


def finish_body(sc, h_ref, *refs):
    pieces, out, lim = refs[:GROUP], refs[GROUP], refs[GROUP + 1]
    lim[...] = pieces[0][TILE:, :].astype(jnp.float32)
    for p, piece in enumerate(pieces):
        half = sc[1] ^ (p >> 1)
        for u in range(2):
            tensor = 2 * (sc[2] ^ (p & 1)) + u
            k = (sc[0] - tensor + N_T) % N_T
            top = lim[pl.ds(k, 1), pl.ds(pl.multiple_of(half * WIDE, TILE), WIDE)]
            first = tensor * 10 + half * (WIDE // TILE)
            for j in range(WIDE // TILE):
                limit = top[:, j * TILE : (j + 1) * TILE]
                value = piece[:TILE, u * WIDE + j * TILE : u * WIDE + (j + 1) * TILE].astype(jnp.float32)
                value = jnp.clip(value, -limit, limit).astype(jnp.bfloat16)
                value = jnp.dot(value, h_ref[...], preferred_element_type=jnp.float32)
                out[:, pl.ds(pl.multiple_of((first + j) * TILE, TILE), TILE)] = value * ROOT


def finish(sc, table, pieces):
    return local(
        finish_body,
        jax.ShapeDtypeStruct((TILE, FULL), jnp.float32),
        1 + GROUP,
        smem=1,
        scratch=[pltpu.VMEM((MORE, BOTH), jnp.float32)],
        cost=cost_of(2 * TILE * TILE * FULL, 4 * MIB),
    )(sc, table, *pieces)


def swap(value, offset):
    return lax.ppermute(value, "dp", [(i, i ^ offset) for i in range(DP)])


def cross(value, offset):
    pairs = [(s * DP + i, (1 - s) * DP + (i ^ offset)) for s in range(2) for i in range(DP)]
    return lax.ppermute(value, ("section", "dp"), pairs)


def along_y(value, steps):
    return lax.ppermute(value, "tensor", [(i, (i + steps) % N_T) for i in range(N_T)])


def along_z(value, steps):
    return lax.ppermute(value, "dp", [(i, (i + steps * GROUP) % DP) for i in range(DP)])


def after(value, *others):
    return lax.optimization_barrier((value, *others))[0]


def limits(expo, perm):
    here = lax.axis_index("tensor")
    top = 448.0 * jnp.exp2(expo.astype(jnp.float32))
    wanted = (here + jnp.arange(N_T, dtype=jnp.int32)) % N_T
    hit = perm[None, :] == wanted[:, None]
    top = jnp.sum(jnp.where(hit[:, :, None], top[None], 0.0), axis=1)
    place = jnp.arange(N_T)[:, None] == jnp.arange(MORE)[None, :]
    rows = jnp.where(place[..., None], top[:, None, :], 0.0)
    return jnp.repeat(rows, TILE, axis=2).astype(jnp.bfloat16)


def chain(values, *others):
    n = len(values)
    return lax.optimization_barrier((*values, *others))[:n]


def shards(left, weight, base, expo, perm):
    table = signs()
    dp = lax.axis_index("dp")
    sc = jnp.concatenate(
        [
            jnp.stack([lax.axis_index("tensor"), (dp // 2) % 2, dp % 2, dp // GROUP]).astype(jnp.int32),
            perm[0, 0],
        ]
    )
    pieces = split_weight(sc, weight[0])
    swapped = [None] + [swap(pieces[p], p) for p in range(1, GROUP)]
    (far,) = order_left(sc, left[0], base[0], True, 1)
    (near,) = order_left(sc, left[0], base[0], False, 1)
    top = limits(expo[0], perm[0, 0])

    held = [{0: join_weight(sc, [pieces[0], swapped[1]])}]
    held[0][7], held[0][1] = along_z(held[0][0], 1), along_z(held[0][0], -1)
    held.append({0: join_weight(sc, chain(swapped[2:], near, far, top))})
    far_x = swap(after(far, held[1][0]), 2)
    near_c = swap(near, 1)
    held[1][7], held[1][1] = along_z(held[1][0], 1), along_z(held[1][0], -1)
    for s in range(2, 4):
        for h in held:
            h[N_Z - s], h[s] = along_z(h[N_Z - s + 1], 1), along_z(h[s - 1], -1)
    held[0][4] = along_z(held[0][5], 1)
    held[1][4] = along_z(held[1][3], -1)

    def begin(parts, i):
        step = 1 if i % 2 == 0 else -1
        return along_y(parts[2], step), along_y(parts[-step], -step), step

    def middle(parts, begun, *wait):
        through, home, step = begun
        through, home = chain((through, home), *wait)
        total = add(parts[step], through)
        return along_y(total, step), home, total

    def end(parts, middled, *wait):
        one, two = chain(middled[:2], *wait)
        return turn(table, [parts[0], one, two])

    own, w = first_product(sc, top, near, [held[side][j] for j in range(N_Z) for side in range(2)])
    own_b = begin(own, 0)
    other = product(sc, near_c, w)
    other_b = begin(other, 1)
    far_x = after(far_x, other[0])
    far_xc = swap(far_x, 1)
    own_m = middle(own, own_b, other[0])
    across = product(sc, after(far_x, own_m[2]), w)
    across_b = begin(across, 0)
    other_m = middle(other, other_b, across[0])
    own_t = end(own, own_m, other_m[2])
    own_x = cross(own_t, 0)
    last = product(sc, after(far_xc, own_t), w)
    last_b = begin(last, 1)
    across_m = middle(across, across_b, last[0])
    other_t = end(other, other_m, across_m[2])
    other_x = cross(other_t, 1)
    last_m = middle(last, last_b, other_t)
    across_t = end(across, across_m, last_m[2], own_x)
    across_x = cross(across_t, 2)
    last_t = end(last, last_m, across_t, other_x)
    return finish(sc, table, (own_x, other_x, across_x, cross(last_t, 3)))[None]


def solution(mesh):
    in_specs = (
        P("section", "dp", "tensor"),
        P("section", ("tensor", "dp"), None),
        P("section", "dp", "tensor"),
        P("section", "dp", "tensor"),
        P("section", "dp", None),
    )
    out_specs = P("section", ("dp", "tensor"), None)
    return jax.shard_map(shards, mesh=mesh, in_specs=in_specs, out_specs=out_specs, check_vma=False)
```

```python
import functools
import math

import jax
import jax.numpy as jnp
import numpy as np
from jax import lax
from jax.experimental import pallas as pl
from jax.experimental.pallas import tpu as pltpu
from jax.sharding import PartitionSpec as P

TILE = 128
N_T = 4
N_Z = 8
GROUP = 4
DP = N_Z * GROUP
WIDE = 640
DEPTH = 2048
FULL = 5120
ROOT = 1.0 / math.sqrt(TILE)
MORE = 16
BOTH = 2 * WIDE
VMEM_LIMIT = 20 * 1024 * 1024
MIB = 1024 * 1024


def signs():
    index = np.arange(TILE)
    common = index[:, None] & index[None, :]
    parity = np.zeros((TILE, TILE), np.int64)
    for shift in range(7):
        parity += (common >> shift) & 1
    return jnp.asarray(1 - 2 * (parity & 1), jnp.bfloat16)


def call(body, out_shape, n_scalar, in_specs, out_specs, grid=(1,), scratch=(), cost=None, vmem=VMEM_LIMIT):
    return pl.pallas_call(
        body,
        out_shape=out_shape,
        grid_spec=pltpu.PrefetchScalarGridSpec(
            num_scalar_prefetch=n_scalar,
            grid=grid,
            in_specs=in_specs,
            out_specs=out_specs,
            scratch_shapes=scratch,
        ),
        compiler_params=pltpu.CompilerParams(vmem_limit_bytes=vmem),
        cost_estimate=cost,
    )


def local(body, out_shape, n_in, smem=0, scratch=(), cost=None):
    vmem = pl.BlockSpec(memory_space=pltpu.VMEM)
    scalar = pl.BlockSpec(memory_space=pltpu.SMEM)
    return pl.pallas_call(
        body,
        out_shape=out_shape,
        in_specs=[scalar] * smem + [vmem] * n_in,
        out_specs=[vmem] * len(out_shape) if isinstance(out_shape, list) else vmem,
        scratch_shapes=scratch,
        compiler_params=pltpu.CompilerParams(vmem_limit_bytes=VMEM_LIMIT),
        cost_estimate=cost,
    )


def cost_of(flops, moved):
    return pl.CostEstimate(flops=flops // 64, bytes_accessed=moved // 64, transcendentals=0)


def bf16(*shape):
    return jax.ShapeDtypeStruct(shape, jnp.bfloat16)


def copy_all(copies, sems):
    started = [pltpu.make_async_copy(src, dst, sems.at[i]) for i, (src, dst) in enumerate(copies)]
    for copy in started:
        copy.start()
    for copy in started:
        copy.wait()


def moving(body, out_shape, n_in, n_copies, cost):
    return pl.pallas_call(
        body,
        out_shape=out_shape,
        in_specs=[pl.BlockSpec(memory_space=pltpu.SMEM)] + [pl.BlockSpec(memory_space=pl.ANY)] * n_in,
        out_specs=jax.tree.map(lambda _: pl.BlockSpec(memory_space=pltpu.VMEM), out_shape),
        scratch_shapes=[pltpu.SemaphoreType.DMA((n_copies,))],
        compiler_params=pltpu.CompilerParams(vmem_limit_bytes=VMEM_LIMIT),
        cost_estimate=cost,
    )


def split_weight_body(sc, w_ref, *refs):
    copies = []
    for p, out in enumerate(refs[:GROUP]):
        for u in range(2):
            start = ((2 * (sc[2] ^ (p & 1)) + u) * 2 + (sc[1] ^ (p >> 1))) * WIDE
            part = w_ref.at[:, pl.ds(pl.multiple_of(start, TILE), WIDE)]
            copies.append((part, out.at[:, pl.ds(u * WIDE, WIDE)]))
    copy_all(copies, refs[GROUP])


def split_weight(sc, weight):
    rows = weight.shape[0]
    return moving(split_weight_body, [bf16(rows, BOTH)] * GROUP, 1, 2 * GROUP, cost_of(0, 4 * rows * FULL))(
        sc, weight
    )


def join_weight_body(sc, *refs):
    rows = refs[0].shape[0]
    for p in range(GROUP):
        start = pl.multiple_of((sc[2] ^ (p & 1)) * rows, rows)
        refs[GROUP + (p >> 1)][pl.ds(start, rows), :] = refs[p][...]


def join_weight(sc, pieces):
    rows = pieces[0].shape[0]
    return local(
        join_weight_body, [bf16(2 * rows, BOTH)] * 2, GROUP, smem=1, cost=cost_of(0, 16 * rows * BOTH)
    )(sc, *pieces)


def order_left_body(sc, left_ref, base_ref, near, far, sems):
    copies = []
    for k in range(N_T):
        j = sum(jnp.where(sc[4 + i] == sc[0] ^ k, i, 0) for i in range(N_T))
        rows = pl.ds(pl.multiple_of(j * TILE, TILE), TILE)
        for out, half in ((far, 1 - sc[1]), (near, sc[1])):
            cols = pl.ds(pl.multiple_of(half * WIDE, TILE), WIDE)
            copies.append((left_ref.at[rows, :], out.at[k, :, pl.ds(0, DEPTH)]))
            copies.append((base_ref.at[rows, cols], out.at[k, :, pl.ds(DEPTH, WIDE)]))
    copy_all(copies, sems)


def order_left(sc, left, base):
    out = bf16(N_T, TILE, DEPTH + WIDE)
    return moving(order_left_body, [out, out], 2, 4 * N_T, cost_of(0, 6 * MIB))(sc, left, base)


KEEP = ((0, 3), (0, 1))
GIVE = ((1, 2), (3, 2))
STEPS = ((1, 3), (3, 1))
PLAIN = 2


def product_body(kind, first, sc, *refs):
    if first:
        top, left, blocks, w, outs = refs[0], refs[1], refs[2 : 2 + 2 * N_Z], refs[-1], refs[2 + 2 * N_Z : -1]
        rows = DEPTH // N_Z // 2
        for j in range(N_Z):
            for side in range(2):
                z = (sc[3] + j) % N_Z
                start = pl.multiple_of((2 * z + (sc[1] ^ side)) * rows, rows)
                w[pl.ds(start, rows), :] = blocks[2 * j + side][...]
    else:
        left, w, outs = refs[0], refs[1], refs[2:]
    if kind == PLAIN:
        pairs = ((0, 1), (2, 3))
        places = [(outs[0].at[...], outs[1].at[...]), (outs[2].at[...], outs[3].at[...])]
    else:
        pairs = (KEEP[kind], GIVE[kind])
        places = [(out.at[0], out.at[1]) for out in outs]
    for pair, place in zip(pairs, places):
        a = jnp.concatenate([left[k, :, :DEPTH] for k in pair], axis=0)
        b = jnp.concatenate([left[k, :, DEPTH:] for k in pair], axis=0).astype(jnp.float32)
        for u in range(2):
            cols = slice(u * WIDE, (u + 1) * WIDE)
            mine = jnp.where((sc[0] == 2 * sc[2] + u), 1.0, 0.0)
            total = jnp.dot(a, w[:, cols], preferred_element_type=jnp.float32)
            total = (total + b * mine).astype(jnp.bfloat16)
            for i, out in enumerate(place):
                out[:TILE, cols] = total[i * TILE : (i + 1) * TILE]
        if first:
            for k, out in zip(pair, place):
                out[TILE:, :] = top[k]


PRODUCT_COST = cost_of(2 * N_T * TILE * DEPTH * BOTH, 8 * MIB)


def first_product(sc, kind, top, left, blocks):
    outs = local(
        functools.partial(product_body, kind, True),
        [bf16(TILE + MORE, BOTH)] * N_T + [bf16(DEPTH, BOTH)],
        2 + len(blocks),
        smem=1,
        cost=PRODUCT_COST,
    )(sc, top, left, *blocks)
    return outs[:N_T], outs[N_T]


def product(sc, kind, left, weight):
    return local(
        functools.partial(product_body, kind, False),
        [bf16(2, TILE, BOTH)] * 2,
        2,
        smem=1,
        cost=PRODUCT_COST,
    )(sc, left, weight)


def add_body(a_ref, b_ref, stay, leave):
    for i, out in enumerate((stay, leave)):
        out[...] = (a_ref[i].astype(jnp.float32) + b_ref[i].astype(jnp.float32)).astype(jnp.bfloat16)


def add(a, b):
    return local(add_body, [bf16(*a.shape[1:])] * 2, 2, cost=cost_of(a.size, 6 * a.size))(a, b)


def turn_body(h_ref, *refs):
    parts, out = refs[:-1], refs[-1]
    for j in range(BOTH // TILE):
        cols = slice(j * TILE, (j + 1) * TILE)
        total = jnp.dot(parts[0][:TILE, cols], h_ref[...], preferred_element_type=jnp.float32)
        for part in parts[1:]:
            total += jnp.dot(part[:TILE, cols], h_ref[...], preferred_element_type=jnp.float32)
        out[:TILE, cols] = (total * ROOT).astype(jnp.bfloat16)
    if out.shape[0] > TILE:
        total = parts[0][TILE:, :].astype(jnp.float32)
        for part in parts[1:]:
            total += part[TILE:, :].astype(jnp.float32)
        out[TILE:, :] = total.astype(jnp.bfloat16)


def turn(table, *parts):
    return local(
        turn_body, bf16(*parts[0].shape), 1 + len(parts), cost=cost_of(4 * TILE * TILE * BOTH, MIB)
    )(table, *parts)


def finish_body(sc, h_ref, *refs):
    pieces, out, lim = refs[:GROUP], refs[GROUP], refs[GROUP + 1]
    lim[...] = pieces[0][TILE:, :].astype(jnp.float32)
    for p, piece in enumerate(pieces):
        half = sc[1] ^ (p >> 1)
        for u in range(2):
            tensor = 2 * (sc[2] ^ (p & 1)) + u
            k = sc[0] ^ tensor
            top = lim[pl.ds(k, 1), pl.ds(pl.multiple_of(half * WIDE, TILE), WIDE)]
            first = tensor * 10 + half * (WIDE // TILE)
            for j in range(WIDE // TILE):
                limit = top[:, j * TILE : (j + 1) * TILE]
                value = piece[:TILE, u * WIDE + j * TILE : u * WIDE + (j + 1) * TILE].astype(jnp.float32)
                value = jnp.clip(value, -limit, limit).astype(jnp.bfloat16)
                value = jnp.dot(value, h_ref[...], preferred_element_type=jnp.float32)
                out[:, pl.ds(pl.multiple_of((first + j) * TILE, TILE), TILE)] = value * ROOT


def finish(sc, table, pieces):
    return local(
        finish_body,
        jax.ShapeDtypeStruct((TILE, FULL), jnp.float32),
        1 + GROUP,
        smem=1,
        scratch=[pltpu.VMEM((MORE, BOTH), jnp.float32)],
        cost=cost_of(2 * TILE * TILE * FULL, 4 * MIB),
    )(sc, table, *pieces)


def swap(value, offset):
    return lax.ppermute(value, "dp", [(i, i ^ offset) for i in range(DP)])


def cross(value, offset):
    pairs = [(s * DP + i, (1 - s) * DP + (i ^ offset)) for s in range(2) for i in range(DP)]
    return lax.ppermute(value, ("section", "dp"), pairs)


def along_y(value, offset):
    return lax.ppermute(value, "tensor", [(i, i ^ offset) for i in range(N_T)])


def along_z(value, steps):
    return lax.ppermute(value, "dp", [(i, (i + steps * GROUP) % DP) for i in range(DP)])


def after(value, *others):
    return lax.optimization_barrier((value, *others))[0]


def limits(expo, perm):
    here = lax.axis_index("tensor")
    top = 448.0 * jnp.exp2(expo.astype(jnp.float32))
    wanted = here ^ jnp.arange(N_T, dtype=jnp.int32)
    hit = perm[None, :] == wanted[:, None]
    top = jnp.sum(jnp.where(hit[:, :, None], top[None], 0.0), axis=1)
    place = jnp.arange(N_T)[:, None] == jnp.arange(MORE)[None, :]
    rows = jnp.where(place[..., None], top[:, None, :], 0.0)
    return jnp.repeat(rows, TILE, axis=2).astype(jnp.bfloat16)


def chain(values, *others):
    n = len(values)
    return lax.optimization_barrier((*values, *others))[:n]


def shards(left, weight, base, expo, perm):
    table = signs()
    dp = lax.axis_index("dp")
    sc = jnp.concatenate(
        [
            jnp.stack([lax.axis_index("tensor"), (dp // 2) % 2, dp % 2, dp // GROUP]).astype(jnp.int32),
            perm[0, 0],
        ]
    )
    pieces = split_weight(sc, weight[0])
    swapped = [None] + [swap(pieces[p], p) for p in range(1, GROUP)]
    top = limits(expo[0], perm[0, 0])

    near, far = order_left(sc, left[0], base[0])
    near_c = swap(near, 1)

    held = [{0: b} for b in join_weight(sc, [pieces[0], *chain(swapped[1:], near, top)])]
    far_x = swap(after(far, held[1][0]), 2)
    for s in range(1, 4):
        for h in held:
            h[N_Z - s], h[s] = along_z(h[(N_Z - s + 1) % N_Z], 1), along_z(h[s - 1], -1)
    held[0][4] = along_z(held[0][5], 1)
    held[1][4] = along_z(held[1][3], -1)

    def begin(parts, kind):
        return parts[0], along_y(parts[1], STEPS[kind][0]), kind

    def middle(begun, *wait):
        keep, got, kind = begun
        (got,) = chain((got,), *wait)
        stay, leave = add(keep, got)
        return stay, along_y(leave, STEPS[kind][1]), leave

    def end(middled, *wait):
        stay, got, _ = middled
        (got,) = chain((got,), *wait)
        return turn(table, stay, got)

    own, w = first_product(sc, PLAIN, top, near, [held[side][j] for j in range(N_Z) for side in range(2)])
    own_got = [along_y(own[k], k) for k in (2, 1, 3)]
    other = begin(product(sc, 0, near_c, w), 0)
    far_x = after(far_x, own[0])
    far_xc = swap(far_x, 1)
    across = begin(product(sc, 1, after(far_x, other[0]), w), 1)
    last = begin(product(sc, 0, after(far_xc, across[0]), w), 0)
    own_t = turn(table, own[0], *chain(own_got, last[0]))
    own_x = cross(own_t, 0)
    other = middle(other, own_t)
    across = middle(across, other[2])
    other_t = end(other, across[2], own_x)
    other_x = cross(other_t, 1)
    across_t = end(across, other_t)
    across_x = cross(across_t, 2)
    last = middle(last, across[2])
    last_t = end(last, across_t, other_x)
    last_x = cross(last_t, 3)
    return finish(sc, table, (own_x, other_x, across_x, last_x))[None]


def solution(mesh):
    in_specs = (
        P("section", "dp", "tensor"),
        P("section", ("tensor", "dp"), None),
        P("section", "dp", "tensor"),
        P("section", "dp", "tensor"),
        P("section", "dp", None),
    )
    out_specs = P("section", ("dp", "tensor"), None)
    return jax.shard_map(shards, mesh=mesh, in_specs=in_specs, out_specs=out_specs, check_vma=False)
```

```python
import functools
import math

import jax
import jax.numpy as jnp
import numpy as np
from jax import lax
from jax.experimental import pallas as pl
from jax.experimental.pallas import tpu as pltpu
from jax.sharding import PartitionSpec as P

TILE = 128
N_T = 4
N_Z = 8
GROUP = 4
DP = N_Z * GROUP
WIDE = 640
DEPTH = 2048
FULL = 5120
ROOT = 1.0 / math.sqrt(TILE)
CONFIG = {'kinds': (2, 0, 1, 0), 'order': ('P0', 'P1', 'P2', 'T0', 'P3', 'M1', 'M2', 'T1', 'M3', 'T2', 'T3'), 'crossed': ((0, 'T1'), (1, 'T3')), 'far': 'P0', 'hold': {}, 'sends': (2, 1, 3)}
MORE = 16
BOTH = 2 * WIDE
VMEM_LIMIT = 20 * 1024 * 1024
MIB = 1024 * 1024


def signs():
    index = np.arange(TILE)
    common = index[:, None] & index[None, :]
    parity = np.zeros((TILE, TILE), np.int64)
    for shift in range(7):
        parity += (common >> shift) & 1
    return jnp.asarray(1 - 2 * (parity & 1), jnp.bfloat16)


def call(body, out_shape, n_scalar, in_specs, out_specs, grid=(1,), scratch=(), cost=None, vmem=VMEM_LIMIT):
    return pl.pallas_call(
        body,
        out_shape=out_shape,
        grid_spec=pltpu.PrefetchScalarGridSpec(
            num_scalar_prefetch=n_scalar,
            grid=grid,
            in_specs=in_specs,
            out_specs=out_specs,
            scratch_shapes=scratch,
        ),
        compiler_params=pltpu.CompilerParams(vmem_limit_bytes=vmem),
        cost_estimate=cost,
    )


def local(body, out_shape, n_in, smem=0, scratch=(), cost=None):
    vmem = pl.BlockSpec(memory_space=pltpu.VMEM)
    scalar = pl.BlockSpec(memory_space=pltpu.SMEM)
    return pl.pallas_call(
        body,
        out_shape=out_shape,
        in_specs=[scalar] * smem + [vmem] * n_in,
        out_specs=[vmem] * len(out_shape) if isinstance(out_shape, list) else vmem,
        scratch_shapes=scratch,
        compiler_params=pltpu.CompilerParams(vmem_limit_bytes=VMEM_LIMIT),
        cost_estimate=cost,
    )


def cost_of(flops, moved):
    return pl.CostEstimate(flops=flops // 64, bytes_accessed=moved // 64, transcendentals=0)


def bf16(*shape):
    return jax.ShapeDtypeStruct(shape, jnp.bfloat16)


def copy_all(copies, sems):
    started = [pltpu.make_async_copy(src, dst, sems.at[i]) for i, (src, dst) in enumerate(copies)]
    for copy in started:
        copy.start()
    for copy in started:
        copy.wait()


def moving(body, out_shape, n_in, n_copies, cost, smem=1, vmem=VMEM_LIMIT):
    return pl.pallas_call(
        body,
        out_shape=out_shape,
        in_specs=[pl.BlockSpec(memory_space=pltpu.SMEM)] * smem + [pl.BlockSpec(memory_space=pl.ANY)] * n_in,
        out_specs=jax.tree.map(lambda _: pl.BlockSpec(memory_space=pltpu.VMEM), out_shape),
        scratch_shapes=[pltpu.SemaphoreType.DMA((n_copies,))],
        compiler_params=pltpu.CompilerParams(vmem_limit_bytes=vmem),
        cost_estimate=cost,
    )


def split_weight_body(w_ref, *refs):
    own = lax.axis_index("dp") % GROUP
    copies = []
    for p, out in enumerate(refs[:GROUP]):
        to = own ^ p
        for u in range(2):
            start = ((2 * (to % 2) + u) * 2 + to // 2) * WIDE
            part = w_ref.at[:, pl.ds(pl.multiple_of(start, TILE), WIDE)]
            copies.append((part, out.at[:, pl.ds(u * WIDE, WIDE)]))
    copy_all(copies, refs[GROUP])


def split_weight(weight):
    rows = weight.shape[0]
    return moving(
        split_weight_body,
        [bf16(rows, BOTH)] * GROUP,
        1,
        2 * GROUP,
        cost_of(0, 4 * rows * FULL),
        smem=0,
        vmem=VMEM_LIMIT,
    )(weight)


def join_weight_body(sc, *refs):
    rows = refs[0].shape[0]
    for p in range(GROUP):
        start = pl.multiple_of((sc[2] ^ (p & 1)) * rows, rows)
        refs[GROUP + (p >> 1)][pl.ds(start, rows), :] = refs[p][...]


def join_weight(sc, pieces):
    rows = pieces[0].shape[0]
    return local(
        join_weight_body, [bf16(2 * rows, BOTH)] * 2, GROUP, smem=1, cost=cost_of(0, 16 * rows * BOTH)
    )(sc, *pieces)


def order_left_body(sc, left_ref, base_ref, near, far, sems):
    copies = []
    for k in range(N_T):
        j = sum(jnp.where(sc[4 + i] == sc[0] ^ k, i, 0) for i in range(N_T))
        rows = pl.ds(pl.multiple_of(j * TILE, TILE), TILE)
        for out, half in ((far, 1 - sc[1]), (near, sc[1])):
            cols = pl.ds(pl.multiple_of(half * WIDE, TILE), WIDE)
            copies.append((left_ref.at[rows, :], out.at[k, :, pl.ds(0, DEPTH)]))
            copies.append((base_ref.at[rows, cols], out.at[k, :, pl.ds(DEPTH, WIDE)]))
    copy_all(copies, sems)


def order_left(sc, left, base):
    out = bf16(N_T, TILE, DEPTH + WIDE)
    return moving(order_left_body, [out, out], 2, 4 * N_T, cost_of(0, 6 * MIB))(sc, left, base)


KEEP = ((0, 3), (0, 1))
GIVE = ((1, 2), (3, 2))
STEPS = ((1, 3), (3, 1))
PLAIN = 2


def product_body(kind, first, sc, *refs):
    if first:
        top, left, blocks, w, outs = refs[0], refs[1], refs[2 : 2 + 2 * N_Z], refs[-1], refs[2 + 2 * N_Z : -1]
        rows = DEPTH // N_Z // 2
        for j in range(N_Z):
            for side in range(2):
                z = (sc[3] + j) % N_Z
                start = pl.multiple_of((2 * z + (sc[1] ^ side)) * rows, rows)
                w[pl.ds(start, rows), :] = blocks[2 * j + side][...]
    else:
        left, w, outs = refs[0], refs[1], refs[2:]
    if kind == PLAIN:
        pairs = ((0, 1), (2, 3))
        places = [(outs[0].at[...], outs[1].at[...]), (outs[2].at[...], outs[3].at[...])]
    else:
        pairs = (KEEP[kind], GIVE[kind])
        places = [(out.at[0], out.at[1]) for out in outs]
    for pair, place in zip(pairs, places):
        a = jnp.concatenate([left[k, :, :DEPTH] for k in pair], axis=0)
        b = jnp.concatenate([left[k, :, DEPTH:] for k in pair], axis=0).astype(jnp.float32)
        for u in range(2):
            cols = slice(u * WIDE, (u + 1) * WIDE)
            mine = jnp.where((sc[0] == 2 * sc[2] + u), 1.0, 0.0)
            total = jnp.dot(a, w[:, cols], preferred_element_type=jnp.float32)
            total = (total + b * mine).astype(jnp.bfloat16)
            for i, out in enumerate(place):
                out[:TILE, cols] = total[i * TILE : (i + 1) * TILE]
        if first:
            for k, out in zip(pair, place):
                out[TILE:, :] = top[k]


PRODUCT_COST = cost_of(2 * N_T * TILE * DEPTH * BOTH, 8 * MIB)


def parts_of(kind, rows):
    return [bf16(rows, BOTH)] * N_T if kind == PLAIN else [bf16(2, rows, BOTH)] * 2


def first_product(sc, kind, top, left, blocks):
    outs = local(
        functools.partial(product_body, kind, True),
        [*parts_of(kind, TILE + MORE), bf16(DEPTH, BOTH)],
        2 + len(blocks),
        smem=1,
        cost=PRODUCT_COST,
    )(sc, top, left, *blocks)
    return outs[:-1], outs[-1]


def product(sc, kind, left, weight):
    return local(
        functools.partial(product_body, kind, False), parts_of(kind, TILE), 2, smem=1, cost=PRODUCT_COST
    )(sc, left, weight)


def add_body(a_ref, b_ref, stay, leave):
    for i, out in enumerate((stay, leave)):
        out[...] = (a_ref[i].astype(jnp.float32) + b_ref[i].astype(jnp.float32)).astype(jnp.bfloat16)


def add(a, b):
    return local(add_body, [bf16(*a.shape[1:])] * 2, 2, cost=cost_of(a.size, 6 * a.size))(a, b)


def turn_body(h_ref, *refs):
    parts, out = refs[:-1], refs[-1]
    for j in range(BOTH // TILE):
        cols = slice(j * TILE, (j + 1) * TILE)
        total = jnp.dot(parts[0][:TILE, cols], h_ref[...], preferred_element_type=jnp.float32)
        for part in parts[1:]:
            total += jnp.dot(part[:TILE, cols], h_ref[...], preferred_element_type=jnp.float32)
        out[:TILE, cols] = (total * ROOT).astype(jnp.bfloat16)
    if out.shape[0] > TILE:
        total = parts[0][TILE:, :].astype(jnp.float32)
        for part in parts[1:]:
            total += part[TILE:, :].astype(jnp.float32)
        out[TILE:, :] = total.astype(jnp.bfloat16)


def turn(table, *parts):
    return local(
        turn_body, bf16(*parts[0].shape), 1 + len(parts), cost=cost_of(4 * TILE * TILE * BOTH, MIB)
    )(table, *parts)


def finish_body(which, sc, h_ref, *refs):
    n = len(which)
    pieces, first_ref, out, done, sems = refs[:n], refs[n], refs[-3], refs[-2], refs[-1]
    lim = first_ref[TILE:, :].astype(jnp.float32)
    copies = []
    for i, (p, piece) in enumerate(zip(which, pieces)):
        half = sc[1] ^ (p >> 1)
        for u in range(2):
            tensor = 2 * (sc[2] ^ (p & 1)) + u
            row = jax.lax.broadcasted_iota(jnp.int32, (MORE, WIDE), 0) == sc[0] ^ tensor
            tops = jnp.where(half == 0, lim[:, :WIDE], lim[:, WIDE:])
            top = jnp.sum(jnp.where(row, tops, 0.0), axis=0, keepdims=True)
            slot = 2 * i + u
            for j in range(WIDE // TILE):
                limit = top[:, j * TILE : (j + 1) * TILE]
                value = piece[:TILE, u * WIDE + j * TILE : u * WIDE + (j + 1) * TILE].astype(jnp.float32)
                value = jnp.clip(value, -limit, limit).astype(jnp.bfloat16)
                value = jnp.dot(value, h_ref[...], preferred_element_type=jnp.float32)
                done[slot, :, j * TILE : (j + 1) * TILE] = value * ROOT
            start = pl.multiple_of((tensor * 2 + half) * WIDE, TILE)
            copies.append(pltpu.make_async_copy(done.at[slot], out.at[:, pl.ds(start, WIDE)], sems.at[slot]))
            copies[-1].start()
    for copy in copies:
        copy.wait()


def finish(sc, table, which, pieces, first, out=None):
    vmem, n = pl.BlockSpec(memory_space=pltpu.VMEM), len(which)
    older = [] if out is None else [out]
    return pl.pallas_call(
        functools.partial(finish_body, which),
        out_shape=jax.ShapeDtypeStruct((TILE, FULL), jnp.float32),
        in_specs=[pl.BlockSpec(memory_space=pltpu.SMEM)] + [vmem] * (2 + n) + [pl.BlockSpec(memory_space=pl.ANY)] * len(older),
        out_specs=pl.BlockSpec(memory_space=pl.ANY),
        scratch_shapes=[pltpu.VMEM((2 * n, TILE, WIDE), jnp.float32), pltpu.SemaphoreType.DMA((2 * n,))],
        input_output_aliases={3 + n: 0} if older else {},
        compiler_params=pltpu.CompilerParams(vmem_limit_bytes=VMEM_LIMIT),
        cost_estimate=cost_of(2 * TILE * TILE * FULL, 4 * MIB),
    )(sc, table, *pieces, first, *older)


def swap(value, offset):
    return lax.ppermute(value, "dp", [(i, i ^ offset) for i in range(DP)])


def cross(value, offset):
    pairs = [(s * DP + i, (1 - s) * DP + (i ^ offset)) for s in range(2) for i in range(DP)]
    return lax.ppermute(value, ("section", "dp"), pairs)


def along_y(value, offset):
    return lax.ppermute(value, "tensor", [(i, i ^ offset) for i in range(N_T)])


def along_z(value, steps):
    return lax.ppermute(value, "dp", [(i, (i + steps * GROUP) % DP) for i in range(DP)])


def after(value, *others):
    return lax.optimization_barrier((value, *others))[0]


def limits(expo, perm):
    here = lax.axis_index("tensor")
    top = 448.0 * jnp.exp2(expo.astype(jnp.float32))
    wanted = here ^ jnp.arange(N_T, dtype=jnp.int32)
    hit = perm[None, :] == wanted[:, None]
    top = jnp.sum(jnp.where(hit[:, :, None], top[None], 0.0), axis=1)
    place = jnp.arange(N_T)[:, None] == jnp.arange(MORE)[None, :]
    rows = jnp.where(place[..., None], top[:, None, :], 0.0)
    return jnp.repeat(rows, TILE, axis=2).astype(jnp.bfloat16)


def chain(values, *others):
    n = len(values)
    return lax.optimization_barrier((*values, *others))[:n]


def shards(left, weight, base, expo, perm):
    table = signs()
    dp = lax.axis_index("dp")
    sc = jnp.concatenate(
        [
            jnp.stack([lax.axis_index("tensor"), (dp // 2) % 2, dp % 2, dp // GROUP]).astype(jnp.int32),
            perm[0, 0],
        ]
    )
    pieces = split_weight(weight[0])
    swapped = [None] + [swap(pieces[p], p) for p in range(1, GROUP)]
    top = limits(expo[0], perm[0, 0])

    near, far = order_left(sc, left[0], base[0])

    held = [{0: b} for b in join_weight(sc, [pieces[0], *chain(swapped[1:], near, far, top)])]
    far_x = swap(after(far, held[1][0]), 2)
    for s in range(1, 4):
        for h in held:
            h[N_Z - s], h[s] = along_z(h[(N_Z - s + 1) % N_Z], 1), along_z(h[s - 1], -1)
    near_c = swap(after(near, held[0][3], held[0][5]), 1)
    held[0][4] = along_z(held[0][5], 1)
    held[1][4] = along_z(held[1][3], -1)

    kinds, order = CONFIG["kinds"], CONFIG["order"]
    parts, sent, far, turned, crossed, outputs = {}, {}, {}, {}, {}, {}
    lefts = {0: near, 1: near_c}
    last = []

    def take(values, name):
        wait = last + [crossed[i] for i, by in CONFIG["crossed"] if by == name]
        return chain(values, *wait) if wait else values

    def send(i, *wait):
        if kinds[i] == PLAIN:
            sent[i] = {k: along_y(*chain((parts[i][k],), *wait), k) for k in CONFIG["sends"]}
        else:
            sent[i] = along_y(*chain((parts[i][1],), *wait), STEPS[kinds[i]][0])

    for name in order:
        step, i = name[0], int(name[1])
        kind = kinds[i]
        if step == "P":
            if i == 0:
                parts[i], w = first_product(sc, kind, top, near, [held[side][j] for j in range(N_Z) for side in range(2)])
            else:
                (left,) = take((lefts[i],), name)
                parts[i] = product(sc, kind, left, w)
            if i not in CONFIG["hold"]:
                send(i)
            mark = parts[i][0]
            if name == CONFIG["far"]:
                lefts[2] = after(far_x, mark)
                lefts[3] = swap(lefts[2], 1)
        elif step == "M":
            (got,) = take((sent[i],), name)
            stay, leave = add(parts[i][0], got)
            far[i] = (stay, along_y(leave, STEPS[kind][1]))
            mark = leave
        else:
            if kind == PLAIN:
                turned[i] = turn(table, parts[i][0], *take([sent[i][k] for k in (1, 2, 3)], name))
            else:
                (got,) = take((far[i][1],), name)
                turned[i] = turn(table, far[i][0], got)
            crossed[i] = cross(turned[i], i)
            mark = turned[i]
        last = [mark]
        for j, by in CONFIG["hold"].items():
            if by == name:
                send(j, mark)
    first, second = chain((crossed[0], crossed[1]), *last), (crossed[2], crossed[3])
    result = finish(sc, table, (0, 1), first, first[0])
    return finish(sc, table, (2, 3), chain(second, result), first[0], result)[None]


def solution(mesh):
    in_specs = (
        P("section", "dp", "tensor"),
        P("section", ("tensor", "dp"), None),
        P("section", "dp", "tensor"),
        P("section", "dp", "tensor"),
        P("section", "dp", None),
    )
    out_specs = P("section", ("dp", "tensor"), None)
    return jax.shard_map(shards, mesh=mesh, in_specs=in_specs, out_specs=out_specs, check_vma=False)
```

```python
import functools
import math

import jax
import jax.numpy as jnp
import numpy as np
from jax import lax
from jax.experimental import pallas as pl
from jax.experimental.pallas import tpu as pltpu
from jax.sharding import PartitionSpec as P

TILE = 128
N_T = 4
N_Z = 8
GROUP = 4
DP = N_Z * GROUP
WIDE = 640
DEPTH = 2048
FULL = 5120
ROOT = 1.0 / math.sqrt(TILE)
CONFIG = {'kinds': (2, 0, 1, 0), 'order': ('P0', 'P1', 'P2', 'T0', 'P3', 'M1', 'M2', 'T1', 'M3', 'T2', 'T3'), 'crossed': ((0, 'T1'), (1, 'T3')), 'far': 'P0', 'hold': {}, 'sends': (2, 1, 3)}
MORE = 16
BOTH = 2 * WIDE
VMEM_LIMIT = 20 * 1024 * 1024
MIB = 1024 * 1024


def signs():
    index = np.arange(TILE)
    common = index[:, None] & index[None, :]
    parity = np.zeros((TILE, TILE), np.int64)
    for shift in range(7):
        parity += (common >> shift) & 1
    return jnp.asarray(1 - 2 * (parity & 1), jnp.bfloat16)


def call(body, out_shape, n_scalar, in_specs, out_specs, grid=(1,), scratch=(), cost=None, vmem=VMEM_LIMIT):
    return pl.pallas_call(
        body,
        out_shape=out_shape,
        grid_spec=pltpu.PrefetchScalarGridSpec(
            num_scalar_prefetch=n_scalar,
            grid=grid,
            in_specs=in_specs,
            out_specs=out_specs,
            scratch_shapes=scratch,
        ),
        compiler_params=pltpu.CompilerParams(vmem_limit_bytes=vmem),
        cost_estimate=cost,
    )


def local(body, out_shape, n_in, smem=0, scratch=(), cost=None):
    vmem = pl.BlockSpec(memory_space=pltpu.VMEM)
    scalar = pl.BlockSpec(memory_space=pltpu.SMEM)
    return pl.pallas_call(
        body,
        out_shape=out_shape,
        in_specs=[scalar] * smem + [vmem] * n_in,
        out_specs=[vmem] * len(out_shape) if isinstance(out_shape, list) else vmem,
        scratch_shapes=scratch,
        compiler_params=pltpu.CompilerParams(vmem_limit_bytes=VMEM_LIMIT),
        cost_estimate=cost,
    )


def cost_of(flops, moved):
    return pl.CostEstimate(flops=flops // 64, bytes_accessed=moved // 64, transcendentals=0)


def bf16(*shape):
    return jax.ShapeDtypeStruct(shape, jnp.bfloat16)


def copy_all(copies, sems):
    started = [pltpu.make_async_copy(src, dst, sems.at[i]) for i, (src, dst) in enumerate(copies)]
    for copy in started:
        copy.start()
    for copy in started:
        copy.wait()


def moving(body, out_shape, n_in, n_copies, cost, smem=1, vmem=VMEM_LIMIT):
    return pl.pallas_call(
        body,
        out_shape=out_shape,
        in_specs=[pl.BlockSpec(memory_space=pltpu.SMEM)] * smem + [pl.BlockSpec(memory_space=pl.ANY)] * n_in,
        out_specs=jax.tree.map(lambda _: pl.BlockSpec(memory_space=pltpu.VMEM), out_shape),
        scratch_shapes=[pltpu.SemaphoreType.DMA((n_copies,))],
        compiler_params=pltpu.CompilerParams(vmem_limit_bytes=vmem),
        cost_estimate=cost,
    )


def split_weight_body(w_ref, *refs):
    own = lax.axis_index("dp") % GROUP
    copies = []
    for p, out in enumerate(refs[:GROUP]):
        to = own ^ p
        for u in range(2):
            start = ((2 * (to % 2) + u) * 2 + to // 2) * WIDE
            part = w_ref.at[:, pl.ds(pl.multiple_of(start, TILE), WIDE)]
            copies.append((part, out.at[:, pl.ds(u * WIDE, WIDE)]))
    copy_all(copies, refs[GROUP])


def split_weight(weight):
    rows = weight.shape[0]
    return moving(
        split_weight_body,
        [bf16(rows, BOTH)] * GROUP,
        1,
        2 * GROUP,
        cost_of(0, 4 * rows * FULL),
        smem=0,
        vmem=VMEM_LIMIT,
    )(weight)


def join_weight_body(sc, *refs):
    rows = refs[0].shape[0]
    for p in range(GROUP):
        start = pl.multiple_of((sc[2] ^ (p & 1)) * rows, rows)
        refs[GROUP + (p >> 1)][pl.ds(start, rows), :] = refs[p][...]


def join_weight(sc, pieces):
    rows = pieces[0].shape[0]
    return local(
        join_weight_body, [bf16(2 * rows, BOTH)] * 2, GROUP, smem=1, cost=cost_of(0, 16 * rows * BOTH)
    )(sc, *pieces)


def order_left_body(sc, left_ref, base_ref, near, far, sems):
    copies = []
    for k in range(N_T):
        j = sum(jnp.where(sc[4 + i] == sc[0] ^ k, i, 0) for i in range(N_T))
        rows = pl.ds(pl.multiple_of(j * TILE, TILE), TILE)
        for out, half in ((far, 1 - sc[1]), (near, sc[1])):
            cols = pl.ds(pl.multiple_of(half * WIDE, TILE), WIDE)
            copies.append((left_ref.at[rows, :], out.at[k, :, pl.ds(0, DEPTH)]))
            copies.append((base_ref.at[rows, cols], out.at[k, :, pl.ds(DEPTH, WIDE)]))
    copy_all(copies, sems)


def order_left(sc, left, base):
    out = bf16(N_T, TILE, DEPTH + WIDE)
    return moving(order_left_body, [out, out], 2, 4 * N_T, cost_of(0, 6 * MIB))(sc, left, base)


KEEP = ((0, 3), (0, 1))
GIVE = ((1, 2), (3, 2))
STEPS = ((1, 3), (3, 1))
PLAIN = 2


def product_body(kind, first, sc, *refs):
    if first:
        top, left, blocks, w, outs = refs[0], refs[1], refs[2 : 2 + 2 * N_Z], refs[-1], refs[2 + 2 * N_Z : -1]
        rows = DEPTH // N_Z // 2
        for j in range(N_Z):
            for side in range(2):
                z = (sc[3] + j) % N_Z
                start = pl.multiple_of((2 * z + (sc[1] ^ side)) * rows, rows)
                w[pl.ds(start, rows), :] = blocks[2 * j + side][...]
    else:
        left, w, outs = refs[0], refs[1], refs[2:]
    if kind == PLAIN:
        pairs = ((0, 1), (2, 3))
        places = [(outs[0].at[...], outs[1].at[...]), (outs[2].at[...], outs[3].at[...])]
    else:
        pairs = (KEEP[kind], GIVE[kind])
        places = [(out.at[0], out.at[1]) for out in outs]
    for pair, place in zip(pairs, places):
        a = jnp.concatenate([left[k, :, :DEPTH] for k in pair], axis=0)
        b = jnp.concatenate([left[k, :, DEPTH:] for k in pair], axis=0).astype(jnp.float32)
        for u in range(2):
            cols = slice(u * WIDE, (u + 1) * WIDE)
            mine = jnp.where((sc[0] == 2 * sc[2] + u), 1.0, 0.0)
            total = jnp.dot(a, w[:, cols], preferred_element_type=jnp.float32)
            total = (total + b * mine).astype(jnp.bfloat16)
            for i, out in enumerate(place):
                out[:TILE, cols] = total[i * TILE : (i + 1) * TILE]
        if first:
            for k, out in zip(pair, place):
                out[TILE:, :] = top[k]


PRODUCT_COST = cost_of(2 * N_T * TILE * DEPTH * BOTH, 8 * MIB)


def parts_of(kind, rows):
    return [bf16(rows, BOTH)] * N_T if kind == PLAIN else [bf16(2, rows, BOTH)] * 2


def first_product(sc, kind, top, left, blocks):
    outs = local(
        functools.partial(product_body, kind, True),
        [*parts_of(kind, TILE + MORE), bf16(DEPTH, BOTH)],
        2 + len(blocks),
        smem=1,
        cost=PRODUCT_COST,
    )(sc, top, left, *blocks)
    return outs[:-1], outs[-1]


def product(sc, kind, left, weight):
    return local(
        functools.partial(product_body, kind, False), parts_of(kind, TILE), 2, smem=1, cost=PRODUCT_COST
    )(sc, left, weight)


def add_body(a_ref, b_ref, stay, leave):
    for i, out in enumerate((stay, leave)):
        out[...] = (a_ref[i].astype(jnp.float32) + b_ref[i].astype(jnp.float32)).astype(jnp.bfloat16)


def add(a, b):
    return local(add_body, [bf16(*a.shape[1:])] * 2, 2, cost=cost_of(a.size, 6 * a.size))(a, b)


def turn_body(h_ref, *refs):
    parts, out = refs[:-1], refs[-1]
    for j in range(BOTH // TILE):
        cols = slice(j * TILE, (j + 1) * TILE)
        total = jnp.dot(parts[0][:TILE, cols], h_ref[...], preferred_element_type=jnp.float32)
        for part in parts[1:]:
            total += jnp.dot(part[:TILE, cols], h_ref[...], preferred_element_type=jnp.float32)
        out[:TILE, cols] = (total * ROOT).astype(jnp.bfloat16)
    if out.shape[0] > TILE:
        total = parts[0][TILE:, :].astype(jnp.float32)
        for part in parts[1:]:
            total += part[TILE:, :].astype(jnp.float32)
        out[TILE:, :] = total.astype(jnp.bfloat16)


def turn(table, *parts):
    return local(
        turn_body, bf16(*parts[0].shape), 1 + len(parts), cost=cost_of(4 * TILE * TILE * BOTH, MIB)
    )(table, *parts)


def finish_body(which, sc, h_ref, *refs):
    n = len(which)
    pieces, first_ref, out, done, sems = refs[:n], refs[n], refs[-3], refs[-2], refs[-1]
    lim = first_ref[TILE:, :].astype(jnp.float32)
    copies = []
    for i, (p, piece) in enumerate(zip(which, pieces)):
        half = sc[1] ^ (p >> 1)
        for u in range(2):
            tensor = 2 * (sc[2] ^ (p & 1)) + u
            row = jax.lax.broadcasted_iota(jnp.int32, (MORE, WIDE), 0) == sc[0] ^ tensor
            tops = jnp.where(half == 0, lim[:, :WIDE], lim[:, WIDE:])
            top = jnp.sum(jnp.where(row, tops, 0.0), axis=0, keepdims=True)
            slot = 2 * i + u
            for j in range(WIDE // TILE):
                limit = top[:, j * TILE : (j + 1) * TILE]
                value = piece[:TILE, u * WIDE + j * TILE : u * WIDE + (j + 1) * TILE].astype(jnp.float32)
                value = jnp.clip(value, -limit, limit).astype(jnp.bfloat16)
                value = jnp.dot(value, h_ref[...], preferred_element_type=jnp.float32)
                done[slot, :, j * TILE : (j + 1) * TILE] = value * ROOT
            start = pl.multiple_of((tensor * 2 + half) * WIDE, TILE)
            copies.append(pltpu.make_async_copy(done.at[slot], out.at[:, pl.ds(start, WIDE)], sems.at[slot]))
            copies[-1].start()
    for copy in copies:
        copy.wait()


def finish(sc, table, which, pieces, first, out=None):
    vmem, n = pl.BlockSpec(memory_space=pltpu.VMEM), len(which)
    older = [] if out is None else [out]
    return pl.pallas_call(
        functools.partial(finish_body, which),
        out_shape=jax.ShapeDtypeStruct((TILE, FULL), jnp.float32),
        in_specs=[pl.BlockSpec(memory_space=pltpu.SMEM)] + [vmem] * (2 + n) + [pl.BlockSpec(memory_space=pl.ANY)] * len(older),
        out_specs=pl.BlockSpec(memory_space=pl.ANY),
        scratch_shapes=[pltpu.VMEM((2 * n, TILE, WIDE), jnp.float32), pltpu.SemaphoreType.DMA((2 * n,))],
        input_output_aliases={3 + n: 0} if older else {},
        compiler_params=pltpu.CompilerParams(vmem_limit_bytes=VMEM_LIMIT),
        cost_estimate=cost_of(2 * TILE * TILE * FULL, 4 * MIB),
    )(sc, table, *pieces, first, *older)


def swap(value, offset):
    return lax.ppermute(value, "dp", [(i, i ^ offset) for i in range(DP)])


def cross(value, offset):
    pairs = [(s * DP + i, (1 - s) * DP + (i ^ offset)) for s in range(2) for i in range(DP)]
    return lax.ppermute(value, ("section", "dp"), pairs)


def along_y(value, offset):
    return lax.ppermute(value, "tensor", [(i, i ^ offset) for i in range(N_T)])


def along_z(value, steps):
    return lax.ppermute(value, "dp", [(i, (i + steps * GROUP) % DP) for i in range(DP)])


def after(value, *others):
    return lax.optimization_barrier((value, *others))[0]


def limits(expo, perm):
    here = lax.axis_index("tensor")
    top = 448.0 * jnp.exp2(expo.astype(jnp.float32))
    wanted = here ^ jnp.arange(N_T, dtype=jnp.int32)
    hit = perm[None, :] == wanted[:, None]
    top = jnp.sum(jnp.where(hit[:, :, None], top[None], 0.0), axis=1)
    place = jnp.arange(N_T)[:, None] == jnp.arange(MORE)[None, :]
    rows = jnp.where(place[..., None], top[:, None, :], 0.0)
    return jnp.repeat(rows, TILE, axis=2).astype(jnp.bfloat16)


def chain(values, *others):
    n = len(values)
    return lax.optimization_barrier((*values, *others))[:n]


def shards(left, weight, base, expo, perm):
    table = signs()
    dp = lax.axis_index("dp")
    sc = jnp.concatenate(
        [
            jnp.stack([lax.axis_index("tensor"), (dp // 2) % 2, dp % 2, dp // GROUP]).astype(jnp.int32),
            perm[0, 0],
        ]
    )
    pieces = split_weight(weight[0])
    swapped = [None] + [swap(pieces[p], p) for p in range(1, GROUP)]
    top = limits(expo[0], perm[0, 0])

    near, far = order_left(sc, left[0], base[0])

    held = [{0: b} for b in join_weight(sc, [pieces[0], *chain(swapped[1:], near, far, top)])]
    far_x = swap(after(far, held[1][0]), 2)
    for s in range(1, 4):
        for h in held:
            h[N_Z - s], h[s] = along_z(h[(N_Z - s + 1) % N_Z], 1), along_z(h[s - 1], -1)
    near_c = swap(after(near, held[0][3], held[0][5]), 1)
    held[0][4] = along_z(held[0][5], 1)
    held[1][4] = along_z(held[1][3], -1)

    kinds, order = CONFIG["kinds"], CONFIG["order"]
    parts, sent, far, turned, crossed, outputs = {}, {}, {}, {}, {}, {}
    lefts = {0: near, 1: near_c}
    last = []

    def take(values, name):
        wait = last + [crossed[i] for i, by in CONFIG["crossed"] if by == name]
        return chain(values, *wait) if wait else values

    def send(i, *wait):
        if kinds[i] == PLAIN:
            sent[i] = {k: along_y(*chain((parts[i][k],), *wait), k) for k in CONFIG["sends"]}
        else:
            sent[i] = along_y(*chain((parts[i][1],), *wait), STEPS[kinds[i]][0])

    for name in order:
        step, i = name[0], int(name[1])
        kind = kinds[i]
        if step == "P":
            if i == 0:
                parts[i], w = first_product(sc, kind, top, near, [held[side][j] for j in range(N_Z) for side in range(2)])
            else:
                (left,) = take((lefts[i],), name)
                parts[i] = product(sc, kind, left, w)
            if i not in CONFIG["hold"]:
                send(i)
            mark = parts[i][0]
            if name == CONFIG["far"]:
                lefts[2] = after(far_x, mark)
                lefts[3] = swap(lefts[2], 1)
        elif step == "M":
            (got,) = take((sent[i],), name)
            stay, leave = add(parts[i][0], got)
            far[i] = (stay, along_y(leave, STEPS[kind][1]))
            mark = leave
        else:
            if kind == PLAIN:
                turned[i] = turn(table, parts[i][0], *take([sent[i][k] for k in (1, 2, 3)], name))
            else:
                (got,) = take((far[i][1],), name)
                turned[i] = turn(table, far[i][0], got)
            crossed[i] = cross(turned[i], i)
            mark = turned[i]
        last = [mark]
        for j, by in CONFIG["hold"].items():
            if by == name:
                send(j, mark)
    first, second = chain((crossed[0], crossed[1]), *last), (crossed[2], crossed[3])
    result = finish(sc, table, (0, 1), first, first[0])
    result = finish(sc, table, (2,), chain(second[:1], result), first[0], result)
    return finish(sc, table, (3,), chain(second[1:], result), first[0], result)[None]


def solution(mesh):
    in_specs = (
        P("section", "dp", "tensor"),
        P("section", ("tensor", "dp"), None),
        P("section", "dp", "tensor"),
        P("section", "dp", "tensor"),
        P("section", "dp", None),
    )
    out_specs = P("section", ("dp", "tensor"), None)
    return jax.shard_map(shards, mesh=mesh, in_specs=in_specs, out_specs=out_specs, check_vma=False)
```

```python
import functools
import math

import jax
import jax.numpy as jnp
import numpy as np
from jax import lax
from jax.experimental import pallas as pl
from jax.experimental.pallas import tpu as pltpu
from jax.sharding import PartitionSpec as P

TILE = 128
N_T = 4
N_Z = 8
GROUP = 4
DP = N_Z * GROUP
WIDE = 640
DEPTH = 2048
FULL = 5120
ROOT = 1.0 / math.sqrt(TILE)
CONFIG = {'kinds': (2, 0, 1, 0), 'order': ('P0', 'P1', 'P2', 'T0', 'P3', 'M1', 'M2', 'T1', 'M3', 'T2', 'T3'), 'crossed': ((0, 'T1'), (1, 'T3')), 'far': 'P0', 'hold': {}, 'sends': (2, 1, 3)}
MORE = 16
BOTH = 2 * WIDE
VMEM_LIMIT = 12 * 1024 * 1024
MIB = 1024 * 1024


def signs():
    index = np.arange(TILE)
    common = index[:, None] & index[None, :]
    parity = np.zeros((TILE, TILE), np.int64)
    for shift in range(7):
        parity += (common >> shift) & 1
    return jnp.asarray(1 - 2 * (parity & 1), jnp.bfloat16)


def call(body, out_shape, n_scalar, in_specs, out_specs, grid=(1,), scratch=(), cost=None, vmem=VMEM_LIMIT):
    return pl.pallas_call(
        body,
        out_shape=out_shape,
        grid_spec=pltpu.PrefetchScalarGridSpec(
            num_scalar_prefetch=n_scalar,
            grid=grid,
            in_specs=in_specs,
            out_specs=out_specs,
            scratch_shapes=scratch,
        ),
        compiler_params=pltpu.CompilerParams(vmem_limit_bytes=vmem),
        cost_estimate=cost,
    )


def local(body, out_shape, n_in, smem=0, scratch=(), cost=None):
    vmem = pl.BlockSpec(memory_space=pltpu.VMEM)
    scalar = pl.BlockSpec(memory_space=pltpu.SMEM)
    return pl.pallas_call(
        body,
        out_shape=out_shape,
        in_specs=[scalar] * smem + [vmem] * n_in,
        out_specs=[vmem] * len(out_shape) if isinstance(out_shape, list) else vmem,
        scratch_shapes=scratch,
        compiler_params=pltpu.CompilerParams(vmem_limit_bytes=VMEM_LIMIT),
        cost_estimate=cost,
    )


def cost_of(flops, moved):
    return pl.CostEstimate(flops=flops // 64, bytes_accessed=moved // 64, transcendentals=0)


def bf16(*shape):
    return jax.ShapeDtypeStruct(shape, jnp.bfloat16)


def copy_all(copies, sems):
    started = [pltpu.make_async_copy(src, dst, sems.at[i]) for i, (src, dst) in enumerate(copies)]
    for copy in started:
        copy.start()
    for copy in started:
        copy.wait()


def moving(body, out_shape, n_in, n_copies, cost, smem=1, vmem=VMEM_LIMIT):
    return pl.pallas_call(
        body,
        out_shape=out_shape,
        in_specs=[pl.BlockSpec(memory_space=pltpu.SMEM)] * smem + [pl.BlockSpec(memory_space=pl.ANY)] * n_in,
        out_specs=jax.tree.map(lambda _: pl.BlockSpec(memory_space=pltpu.VMEM), out_shape),
        scratch_shapes=[pltpu.SemaphoreType.DMA((n_copies,))],
        compiler_params=pltpu.CompilerParams(vmem_limit_bytes=vmem),
        cost_estimate=cost,
    )


def split_weight_body(w_ref, *refs):
    own = lax.axis_index("dp") % GROUP
    copies = []
    for p, out in enumerate(refs[:GROUP]):
        to = own ^ p
        for u in range(2):
            start = ((2 * (to % 2) + u) * 2 + to // 2) * WIDE
            part = w_ref.at[:, pl.ds(pl.multiple_of(start, TILE), WIDE)]
            copies.append((part, out.at[:, pl.ds(u * WIDE, WIDE)]))
    copy_all(copies, refs[GROUP])


def split_weight(weight):
    rows = weight.shape[0]
    return moving(
        split_weight_body,
        [bf16(rows, BOTH)] * GROUP,
        1,
        2 * GROUP,
        cost_of(0, 4 * rows * FULL),
        smem=0,
        vmem=VMEM_LIMIT,
    )(weight)


def join_weight_body(sc, *refs):
    rows = refs[0].shape[0]
    for p in range(GROUP):
        start = pl.multiple_of((sc[2] ^ (p & 1)) * rows, rows)
        refs[GROUP + (p >> 1)][pl.ds(start, rows), :] = refs[p][...]


def join_weight(sc, pieces):
    rows = pieces[0].shape[0]
    return local(
        join_weight_body, [bf16(2 * rows, BOTH)] * 2, GROUP, smem=1, cost=cost_of(0, 16 * rows * BOTH)
    )(sc, *pieces)


def order_left_body(sc, left_ref, base_ref, near, far, sems):
    copies = []
    for k in range(N_T):
        j = sum(jnp.where(sc[4 + i] == sc[0] ^ k, i, 0) for i in range(N_T))
        rows = pl.ds(pl.multiple_of(j * TILE, TILE), TILE)
        for out, half in ((far, 1 - sc[1]), (near, sc[1])):
            cols = pl.ds(pl.multiple_of(half * WIDE, TILE), WIDE)
            copies.append((left_ref.at[rows, :], out.at[k, :, pl.ds(0, DEPTH)]))
            copies.append((base_ref.at[rows, cols], out.at[k, :, pl.ds(DEPTH, WIDE)]))
    copy_all(copies, sems)


def order_left(sc, left, base):
    out = bf16(N_T, TILE, DEPTH + WIDE)
    return moving(order_left_body, [out, out], 2, 4 * N_T, cost_of(0, 6 * MIB))(sc, left, base)


KEEP = ((0, 3), (0, 1))
GIVE = ((1, 2), (3, 2))
STEPS = ((1, 3), (3, 1))
PLAIN = 2


def product_body(kind, first, sc, *refs):
    if first:
        top, left, blocks, w, outs = refs[0], refs[1], refs[2 : 2 + 2 * N_Z], refs[-1], refs[2 + 2 * N_Z : -1]
        rows = DEPTH // N_Z // 2
        for j in range(N_Z):
            for side in range(2):
                z = (sc[3] + j) % N_Z
                start = pl.multiple_of((2 * z + (sc[1] ^ side)) * rows, rows)
                w[pl.ds(start, rows), :] = blocks[2 * j + side][...]
    else:
        left, w, outs = refs[0], refs[1], refs[2:]
    if kind == PLAIN:
        pairs = ((0, 1), (2, 3))
        places = [(outs[0].at[...], outs[1].at[...]), (outs[2].at[...], outs[3].at[...])]
    else:
        pairs = (KEEP[kind], GIVE[kind])
        places = [(out.at[0], out.at[1]) for out in outs]
    for pair, place in zip(pairs, places):
        a = jnp.concatenate([left[k, :, :DEPTH] for k in pair], axis=0)
        b = jnp.concatenate([left[k, :, DEPTH:] for k in pair], axis=0).astype(jnp.float32)
        for u in range(2):
            cols = slice(u * WIDE, (u + 1) * WIDE)
            mine = jnp.where((sc[0] == 2 * sc[2] + u), 1.0, 0.0)
            total = jnp.dot(a, w[:, cols], preferred_element_type=jnp.float32)
            total = (total + b * mine).astype(jnp.bfloat16)
            for i, out in enumerate(place):
                out[:TILE, cols] = total[i * TILE : (i + 1) * TILE]
        if first:
            for k, out in zip(pair, place):
                out[TILE:, :] = top[k]


PRODUCT_COST = cost_of(2 * N_T * TILE * DEPTH * BOTH, 8 * MIB)


def parts_of(kind, rows):
    return [bf16(rows, BOTH)] * N_T if kind == PLAIN else [bf16(2, rows, BOTH)] * 2


def first_product(sc, kind, top, left, blocks):
    outs = local(
        functools.partial(product_body, kind, True),
        [*parts_of(kind, TILE + MORE), bf16(DEPTH, BOTH)],
        2 + len(blocks),
        smem=1,
        cost=PRODUCT_COST,
    )(sc, top, left, *blocks)
    return outs[:-1], outs[-1]


def product(sc, kind, left, weight):
    return local(
        functools.partial(product_body, kind, False), parts_of(kind, TILE), 2, smem=1, cost=PRODUCT_COST
    )(sc, left, weight)


def add_body(a_ref, b_ref, stay, leave):
    for i, out in enumerate((stay, leave)):
        out[...] = (a_ref[i].astype(jnp.float32) + b_ref[i].astype(jnp.float32)).astype(jnp.bfloat16)


def add(a, b):
    return local(add_body, [bf16(*a.shape[1:])] * 2, 2, cost=cost_of(a.size, 6 * a.size))(a, b)


def turn_body(h_ref, *refs):
    parts, out = refs[:-1], refs[-1]
    for j in range(BOTH // TILE):
        cols = slice(j * TILE, (j + 1) * TILE)
        total = jnp.dot(parts[0][:TILE, cols], h_ref[...], preferred_element_type=jnp.float32)
        for part in parts[1:]:
            total += jnp.dot(part[:TILE, cols], h_ref[...], preferred_element_type=jnp.float32)
        out[:TILE, cols] = (total * ROOT).astype(jnp.bfloat16)
    if out.shape[0] > TILE:
        total = parts[0][TILE:, :].astype(jnp.float32)
        for part in parts[1:]:
            total += part[TILE:, :].astype(jnp.float32)
        out[TILE:, :] = total.astype(jnp.bfloat16)


def turn(table, *parts):
    return local(
        turn_body, bf16(*parts[0].shape), 1 + len(parts), cost=cost_of(4 * TILE * TILE * BOTH, MIB)
    )(table, *parts)


def finish_body(which, sc, h_ref, *refs):
    n = len(which)
    pieces, first_ref, out, done, sems = refs[:n], refs[n], refs[-3], refs[-2], refs[-1]
    lim = first_ref[TILE:, :].astype(jnp.float32)
    copies = []
    for i, (p, piece) in enumerate(zip(which, pieces)):
        half = sc[1] ^ (p >> 1)
        for u in range(2):
            tensor = 2 * (sc[2] ^ (p & 1)) + u
            row = jax.lax.broadcasted_iota(jnp.int32, (MORE, WIDE), 0) == sc[0] ^ tensor
            tops = jnp.where(half == 0, lim[:, :WIDE], lim[:, WIDE:])
            top = jnp.sum(jnp.where(row, tops, 0.0), axis=0, keepdims=True)
            slot = 2 * i + u
            for j in range(WIDE // TILE):
                limit = top[:, j * TILE : (j + 1) * TILE]
                value = piece[:TILE, u * WIDE + j * TILE : u * WIDE + (j + 1) * TILE].astype(jnp.float32)
                value = jnp.clip(value, -limit, limit).astype(jnp.bfloat16)
                value = jnp.dot(value, h_ref[...], preferred_element_type=jnp.float32)
                done[slot, :, j * TILE : (j + 1) * TILE] = value * ROOT
            start = pl.multiple_of((tensor * 2 + half) * WIDE, TILE)
            copies.append(pltpu.make_async_copy(done.at[slot], out.at[:, pl.ds(start, WIDE)], sems.at[slot]))
            copies[-1].start()
    for copy in copies:
        copy.wait()


def finish(sc, table, which, pieces, first, out=None):
    vmem, n = pl.BlockSpec(memory_space=pltpu.VMEM), len(which)
    older = [] if out is None else [out]
    return pl.pallas_call(
        functools.partial(finish_body, which),
        out_shape=jax.ShapeDtypeStruct((TILE, FULL), jnp.float32),
        in_specs=[pl.BlockSpec(memory_space=pltpu.SMEM)] + [vmem] * (2 + n) + [pl.BlockSpec(memory_space=pl.ANY)] * len(older),
        out_specs=pl.BlockSpec(memory_space=pl.ANY),
        scratch_shapes=[pltpu.VMEM((2 * n, TILE, WIDE), jnp.float32), pltpu.SemaphoreType.DMA((2 * n,))],
        input_output_aliases={3 + n: 0} if older else {},
        compiler_params=pltpu.CompilerParams(vmem_limit_bytes=VMEM_LIMIT),
        cost_estimate=cost_of(2 * TILE * TILE * FULL, 4 * MIB),
    )(sc, table, *pieces, first, *older)


def swap(value, offset):
    return lax.ppermute(value, "dp", [(i, i ^ offset) for i in range(DP)])


def cross(value, offset):
    pairs = [(s * DP + i, (1 - s) * DP + (i ^ offset)) for s in range(2) for i in range(DP)]
    return lax.ppermute(value, ("section", "dp"), pairs)


def along_y(value, offset):
    return lax.ppermute(value, "tensor", [(i, i ^ offset) for i in range(N_T)])


def along_z(value, steps):
    return lax.ppermute(value, "dp", [(i, (i + steps * GROUP) % DP) for i in range(DP)])


def after(value, *others):
    return lax.optimization_barrier((value, *others))[0]


def limits(expo, perm):
    here = lax.axis_index("tensor")
    top = 448.0 * jnp.exp2(expo.astype(jnp.float32))
    wanted = here ^ jnp.arange(N_T, dtype=jnp.int32)
    hit = perm[None, :] == wanted[:, None]
    top = jnp.sum(jnp.where(hit[:, :, None], top[None], 0.0), axis=1)
    place = jnp.arange(N_T)[:, None] == jnp.arange(MORE)[None, :]
    rows = jnp.where(place[..., None], top[:, None, :], 0.0)
    return jnp.repeat(rows, TILE, axis=2).astype(jnp.bfloat16)


def chain(values, *others):
    n = len(values)
    return lax.optimization_barrier((*values, *others))[:n]


def shards(left, weight, base, expo, perm):
    table = signs()
    dp = lax.axis_index("dp")
    sc = jnp.concatenate(
        [
            jnp.stack([lax.axis_index("tensor"), (dp // 2) % 2, dp % 2, dp // GROUP]).astype(jnp.int32),
            perm[0, 0],
        ]
    )
    pieces = split_weight(weight[0])
    swapped = [None] + [swap(pieces[p], p) for p in range(1, GROUP)]
    top = limits(expo[0], perm[0, 0])

    near, far = order_left(sc, left[0], base[0])

    held = [{0: b} for b in join_weight(sc, [pieces[0], *chain(swapped[1:], near, far, top)])]
    far_x = swap(after(far, held[1][0]), 2)
    for s in range(1, 4):
        for h in held:
            h[N_Z - s], h[s] = along_z(h[(N_Z - s + 1) % N_Z], 1), along_z(h[s - 1], -1)
    near_c = swap(after(near, held[0][3], held[0][5]), 1)
    held[0][4] = along_z(held[0][5], 1)
    held[1][4] = along_z(held[1][3], -1)

    kinds, order = CONFIG["kinds"], CONFIG["order"]
    parts, sent, far, turned, crossed, outputs = {}, {}, {}, {}, {}, {}
    lefts = {0: near, 1: near_c}
    last = []

    def take(values, name):
        wait = last + [crossed[i] for i, by in CONFIG["crossed"] if by == name]
        return chain(values, *wait) if wait else values

    def send(i, *wait):
        if kinds[i] == PLAIN:
            sent[i] = {k: along_y(*chain((parts[i][k],), *wait), k) for k in CONFIG["sends"]}
        else:
            sent[i] = along_y(*chain((parts[i][1],), *wait), STEPS[kinds[i]][0])

    for name in order:
        step, i = name[0], int(name[1])
        kind = kinds[i]
        if step == "P":
            if i == 0:
                parts[i], w = first_product(sc, kind, top, near, [held[side][j] for j in range(N_Z) for side in range(2)])
            else:
                (left,) = take((lefts[i],), name)
                parts[i] = product(sc, kind, left, w)
            if i not in CONFIG["hold"]:
                send(i)
            mark = parts[i][0]
            if name == CONFIG["far"]:
                lefts[2] = after(far_x, mark)
                lefts[3] = swap(lefts[2], 1)
        elif step == "M":
            (got,) = take((sent[i],), name)
            stay, leave = add(parts[i][0], got)
            far[i] = (stay, along_y(leave, STEPS[kind][1]))
            mark = leave
        else:
            if kind == PLAIN:
                turned[i] = turn(table, parts[i][0], *take([sent[i][k] for k in (1, 2, 3)], name))
            else:
                (got,) = take((far[i][1],), name)
                turned[i] = turn(table, far[i][0], got)
            crossed[i] = cross(turned[i], i)
            mark = turned[i]
        last = [mark]
        for j, by in CONFIG["hold"].items():
            if by == name:
                send(j, mark)
    first, second = chain((crossed[0], crossed[1]), *last), (crossed[2], crossed[3])
    result = finish(sc, table, (0, 1), first, first[0])
    result = finish(sc, table, (2,), chain(second[:1], result), first[0], result)
    return finish(sc, table, (3,), chain(second[1:], result), first[0], result)[None]


def solution(mesh):
    in_specs = (
        P("section", "dp", "tensor"),
        P("section", ("tensor", "dp"), None),
        P("section", "dp", "tensor"),
        P("section", "dp", "tensor"),
        P("section", "dp", None),
    )
    out_specs = P("section", ("dp", "tensor"), None)
    return jax.shard_map(shards, mesh=mesh, in_specs=in_specs, out_specs=out_specs, check_vma=False)
```
